256 devices in a mesh: ex: 32 (over y_lo, z, core), feat: 8 (over y_hi, x).
Axes of the slice: x: 4, y: 4 (y_hi: 2, y_lo: 2; y = y_hi * 2 + y_lo), z: 8, core: 2. Of those that a mesh axis runs over, the one named last changes fastest.
Arguments:
- examples: bfloat16 [16384, 8192], P('ex', 'feat'), may hold values from -0.06591797 to 0.06591797
Outputs:
- bands: float32 [17, 16384, 512], P(None, ('ex', 'feat'))
The draws below stay inside these ranges and needn't reach their ends.
All inputs are finite; a program needn't handle non-finite values.
Results may differ from the reference program's by a relative error of at most 0.0003.
Values may be sent and summed in bfloat16 or wider, within the bound.
No kernel may reach another device: no remote copies, remote signals or barrier semaphores. Data moves between devices by JAX's collectives and lax.ppermute only.
A program may use at most 128 MiB of HBM per device.

```python
import jax
import jax.numpy as jnp

F = 8192
E_DEV = 512
NTOT = 16384
N_EX = 32


def level_of(key, dims, shards, smallest, high):
    factor_of, own = 1.0, jax.random.fold_in(key, 6)
    for dim, shards_of in shards:
        draws = jnp.exp(jax.random.uniform(jax.random.fold_in(own, dim), (shards_of,), jnp.float32, smallest / len(shards), high / len(shards)))
        factor_of = factor_of * jnp.repeat(draws, dims[dim] // shards_of).reshape([-1 if axis == dim else 1 for axis in range(len(dims))])
    return factor_of


def normal_values(key, shape, deviation, reach, shards=(), dtype=jnp.bfloat16):
    drawn = jax.random.normal(key, shape, jnp.float32) * deviation
    if len(shards) > 0:
        drawn = level_of(key, shape, shards, -0.22, 0.18) * drawn
    return jnp.clip(drawn, min=-reach, max=reach).astype(dtype)


def setup_inputs(seed: int = 0) -> dict:
    key_of = jax.random.split(jax.random.key(seed), 2)
    return {
        "examples": normal_values(key_of[0], (NTOT, F), (F ** -0.5), 0.06591797, ((0, 32), (1, 8))),
    }


def reference(examples):
    blocks = examples.astype(jnp.float32).reshape(N_EX, E_DEV, F)
    stacked = []
    for offset in range(N_EX // 2 + 1):
        others = jnp.roll(blocks, -offset, axis=0)
        tiles = jnp.einsum("icf,irf->icr", others, blocks)
        stacked.append(tiles.reshape(NTOT, E_DEV))
    return jnp.stack(stacked, axis=0)
```

```python
import jax
import jax.numpy as jnp
from jax import lax
from jax.experimental import pallas as pl
from jax.experimental.pallas import tpu as pltpu
from jax.sharding import PartitionSpec as P


def tiles_kernel(full_ref, *refs):
    slice_refs, out_ref = refs[:-1], refs[-1]
    rows = jnp.concatenate([ref[0] for ref in slice_refs], axis=0)
    product = lax.dot_general(
        rows, full_ref[0], (((1,), (1,)), ((), ())), preferred_element_type=jnp.float32
    )
    product = product.reshape(out_ref.shape)

    @pl.when(pl.program_id(0) == 0)
    def _():
        out_ref[...] = product

    @pl.when(pl.program_id(0) > 0)
    def _():
        out_ref[...] += product


def tiles(full, slices):
    parts, wide, depth = full.shape
    rows = slices[0].shape[1]
    count = len(slices)
    return pl.pallas_call(
        tiles_kernel,
        grid=(parts,),
        in_specs=[pl.BlockSpec((1, wide, depth), lambda f: (f, 0, 0))]
        + [pl.BlockSpec((1, rows, depth), lambda f: (f, 0, 0))] * count,
        out_specs=pl.BlockSpec((count, rows, wide), lambda f: (0, 0, 0)),
        out_shape=jax.ShapeDtypeStruct((count, rows, wide), jnp.float32),
        compiler_params=pltpu.CompilerParams(vmem_limit_bytes=24 * 1024 * 1024),
        cost_estimate=pl.CostEstimate(
            flops=2 * parts * wide * depth * rows * count,
            bytes_accessed=2 * parts * depth * (wide + rows * count) + 4 * count * rows * wide,
            transcendentals=0,
        ),
    )(full, *slices)


def per_device(examples):
    blocks = lax.axis_size("ex")
    feats = lax.axis_size("feat")
    half = blocks // 2
    steps = blocks // 8
    core = lax.axis_index("ex") % 2
    rows, depth = examples.shape

    full = lax.all_gather(examples, "feat", axis=0)
    own = lax.all_to_all(examples.reshape(feats, rows // feats, depth), "feat", 0, 0)

    swap_pairs = [(i, i ^ 1) for i in range(blocks)]
    first_pairs = [(i, (i - 2) % blocks if i % 2 == 0 else (i + half) % blocks) for i in range(blocks)]
    later_pairs = [(i, (i - 2) % blocks if i % 2 == 0 else (i + 2) % blocks) for i in range(blocks)]

    other = lax.ppermute(own, "ex", swap_pairs)
    found = tiles(full, [own, other])
    even = jnp.where(core == 0, found[0], found[1])
    odd = jnp.where(core == 0, found[1], found[0])
    table = [None] * (half + 2)
    table[0], table[1] = even, odd
    held = [own, other]
    for step in range(1, steps + 1):
        pairs = first_pairs if step == 1 else later_pairs
        held = [lax.ppermute(piece, "ex", pairs) for piece in held]
        across = [lax.ppermute(piece, "ex", swap_pairs) for piece in held]
        found = tiles(full, held + across)
        low, high = step, half // 2 + 1 - step
        table[2 * low] = jnp.where(core == 0, found[0], found[2])
        table[2 * low + 1] = jnp.where(core == 0, found[1], found[3])
        table[2 * high + 1] = jnp.where(core == 0, found[2], found[0])
        table[2 * high] = jnp.where(core == 0, found[3], found[1])
    return jnp.where(core == 0, jnp.stack(table[:-1]), jnp.stack(table[1:]))


def solution(mesh):
    placed = (P("ex", "feat"),)
    return jax.shard_map(
        per_device,
        mesh=mesh,
        in_specs=placed,
        out_specs=P(None, ("ex", "feat"), None),
        check_vma=False,
    )
```

```python
import functools

import jax
import jax.numpy as jnp
from jax import lax
from jax.experimental import pallas as pl
from jax.experimental.pallas import tpu as pltpu
from jax.sharding import PartitionSpec as P

ROWS_LAST = (((1,), (1,)), ((), ()))


def after(value, *others):
    return lax.optimization_barrier((value, *others))[0]


def tiles_kernel(sizes, aliased, place_ref, *refs):
    pieces = sum(sizes)
    full_refs, piece_refs = refs[:2], refs[2 : 2 + 2 * pieces]
    out_ref = refs[2 + 2 * pieces + aliased]
    full, held, found, full_sem, held_sem, out_sem = refs[3 + 2 * pieces + aliased :]
    parts = full_refs[0].shape[0]
    count = held.shape[2]
    rows = count // 2

    full_copies = [
        pltpu.make_async_copy(full_refs[h].at[f], full.at[h * parts + f], full_sem.at[h * parts + f])
        for h in range(2)
        for f in range(parts)
    ]
    held_copies = [
        pltpu.make_async_copy(piece_refs[2 * i + h], held.at[i, pl.ds(h * parts, parts)], held_sem.at[2 * i + h])
        for i in range(pieces)
        for h in range(2)
    ]
    first = 2 * sizes[0]
    full_copies[0].start()
    for copy in held_copies[:first:2]:
        copy.start()
    for copy in full_copies[1:parts]:
        copy.start()
    for copy in held_copies[1:first:2]:
        copy.start()
    for copy in full_copies[parts:] + held_copies[first:]:
        copy.start()

    def out_copy(tile):
        return pltpu.make_async_copy(found.at[pl.ds(tile * rows, rows)], out_ref.at[place_ref[tile]], out_sem.at[tile])

    base = 0
    for g, size in enumerate(sizes):
        total = None
        for f in range(2 * parts):
            if g == 0:
                full_copies[f].wait()
            if f % parts == 0:
                for copy in held_copies[2 * base + f // parts : 2 * (base + size) : 2]:
                    copy.wait()
            lhs = jnp.concatenate([held[base + i, f] for i in range(size)], axis=0)
            part = lax.dot_general(lhs, full[f], ROWS_LAST, preferred_element_type=jnp.float32)
            total = part if total is None else total + part
        found[pl.ds(base * count, size * count)] = total
        for tile in range(2 * base, 2 * (base + size)):

            @pl.when(place_ref[tile] >= 0)
            def _(tile=tile):
                out_copy(tile).start()

        base += size
    for tile in range(2 * pieces):

        @pl.when(place_ref[tile] >= 0)
        def _(tile=tile):
            out_copy(tile).wait()


def tiles(place, near, far, groups, shape, out=None):
    parts, wide, depth = near.shape
    sizes = tuple(len(group) for group in groups)
    pieces = [half for group in groups for piece in group for half in piece]
    number = len(pieces) // 2
    count = pieces[0].shape[1]
    anywhere = pl.BlockSpec(memory_space=pl.ANY)
    given = [place, near, far, *pieces] + ([] if out is None else [out])
    return pl.pallas_call(
        functools.partial(tiles_kernel, sizes, 0 if out is None else 1),
        in_specs=[pl.BlockSpec(memory_space=pltpu.SMEM)] + [anywhere] * (len(given) - 1),
        out_specs=anywhere,
        out_shape=jax.ShapeDtypeStruct(shape, jnp.float32),
        input_output_aliases={} if out is None else {len(given) - 1: 0},
        scratch_shapes=[
            pltpu.VMEM((2 * parts, wide, depth), near.dtype),
            pltpu.VMEM((number, 2 * parts, count, depth), near.dtype),
            pltpu.VMEM((number * count, wide), jnp.float32),
            pltpu.SemaphoreType.DMA((2 * parts,)),
            pltpu.SemaphoreType.DMA((2 * number,)),
            pltpu.SemaphoreType.DMA((2 * number,)),
        ],
        compiler_params=pltpu.CompilerParams(vmem_limit_bytes=52 * 1024 * 1024),
        cost_estimate=pl.CostEstimate(
            flops=4 * parts * wide * depth * number * count,
            bytes_accessed=4 * parts * depth * (wide + number * count) + 4 * number * count * wide,
            transcendentals=0,
        ),
    )(*given)


def per_device(examples):
    blocks = lax.axis_size("ex")
    feats = lax.axis_size("feat")
    half = blocks // 2
    steps = blocks // 8
    ex = lax.axis_index("ex")
    core = ex % 2
    rows, depth = examples.shape
    line = feats // 2
    lines = [[q * line + x for x in range(line)] for q in range(2)]

    swap_pairs = [(i, i ^ 1) for i in range(blocks)]
    first_pairs = [(i, i - 2) for i in range(blocks) if i % 2 == 0 and i % half != 0]
    first_pairs += [(i, (i + half) % blocks) for i in range(blocks) if i % 2 == 1]
    wrap_pairs = [(1, half - 2), (half + 1, blocks - 2)]
    later_pairs = [(i, (i - 2 if i % 2 == 0 else i + 2) % blocks) for i in range(blocks)]
    wraps = (core == 0) & (ex % half == half - 2)

    def swap(piece):
        return lax.ppermute(piece, "ex", swap_pairs)

    near = lax.all_gather(examples, "feat", axis=0, axis_index_groups=lines)
    facing = lax.ppermute(examples, "feat", [(f, (f + line) % feats) for f in range(feats)])
    own = lax.all_to_all(examples.reshape(feats, rows // feats, depth), "feat", 0, 0)
    first = lax.axis_index("feat") < line
    own = after(own, facing)
    own_halves = [jnp.where(first, own[:line], own[line:]), jnp.where(first, own[line:], own[:line])]
    start = [jnp.concatenate([piece, swap(piece)], axis=1) for piece in own_halves]

    spots = [jnp.where(core == 0, 0, 1), jnp.where(core == 0, 1, 0)]
    for step in range(1, steps + 1):
        low, high = 2 * step, half + 2 - 2 * step
        mine, theirs = jnp.where(core == 0, low, high), jnp.where(core == 0, high, low)
        spots += [mine + core, mine + 1 - core, theirs + 1 - core, theirs + core]
    place = jnp.stack([jnp.where(spot - core > half, -1, spot - core) for spot in spots]).astype(jnp.int32)
    shape = (half + 1, rows // feats, rows)
    split = 2 + 4 * (steps - 1)

    turn = rows // feats
    held = start
    groups = [[start]]
    for step in range(steps):
        if step == 2:
            held = [after(held[0], near), held[1]]
        held = [lax.ppermute(piece, "ex", first_pairs if step == 0 else later_pairs) for piece in held]
        if step == 0:
            wrapped = [lax.ppermute(piece, "ex", wrap_pairs) for piece in held]
            held = [
                jnp.where(wraps, jnp.concatenate([new[:, turn:], new[:, :turn]], axis=1), piece)
                for new, piece in zip(wrapped, held)
            ]
            far = lax.all_gather(facing, "feat", axis=0, axis_index_groups=lines)
        if step == steps - 1:
            out = tiles(place[:split], near, far, groups, shape)
            held = [held[0], after(held[1], out)]
        groups.append([held, [swap(piece) for piece in held]])

    return tiles(place[split:], near, far, groups[-1:], shape, out)


def solution(mesh):
    placed = (P("ex", "feat"),)
    return jax.shard_map(
        per_device,
        mesh=mesh,
        in_specs=placed,
        out_specs=P(None, ("ex", "feat"), None),
        check_vma=False,
    )
```

```python
import functools

import jax
import jax.numpy as jnp
from jax import lax
from jax.experimental import pallas as pl
from jax.experimental.pallas import tpu as pltpu
from jax.sharding import PartitionSpec as P

ROWS_LAST = (((1,), (1,)), ((), ()))


def after(value, *others):
    return lax.optimization_barrier((value, *others))[0]


def tiles_kernel(sizes, aliased, place_ref, *refs):
    pieces = sum(sizes)
    full_refs, piece_refs = refs[:2], refs[2 : 2 + 2 * pieces]
    out_ref = refs[2 + 2 * pieces + aliased]
    full, held, found, full_sem, held_sem, out_sem = refs[3 + 2 * pieces + aliased :]
    parts = full_refs[0].shape[0]
    count = held.shape[2]
    rows = count // 2

    full_copies = [
        pltpu.make_async_copy(full_refs[h].at[f], full.at[h * parts + f], full_sem.at[h * parts + f])
        for h in range(2)
        for f in range(parts)
    ]
    held_copies = [
        pltpu.make_async_copy(piece_refs[2 * i + h], held.at[i, pl.ds(h * parts, parts)], held_sem.at[2 * i + h])
        for i in range(pieces)
        for h in range(2)
    ]
    first = 2 * sizes[0]
    full_copies[0].start()
    for copy in held_copies[:first:2]:
        copy.start()
    for copy in full_copies[1:parts]:
        copy.start()
    for copy in held_copies[1:first:2]:
        copy.start()
    for copy in full_copies[parts:] + held_copies[first:]:
        copy.start()

    def out_copy(tile):
        return pltpu.make_async_copy(found.at[pl.ds(tile * rows, rows)], out_ref.at[place_ref[tile]], out_sem.at[tile])

    base = 0
    for g, size in enumerate(sizes):
        total = None
        for f in range(2 * parts):
            if g == 0:
                full_copies[f].wait()
            if f % parts == 0:
                for copy in held_copies[2 * base + f // parts : 2 * (base + size) : 2]:
                    copy.wait()
            lhs = jnp.concatenate([held[base + i, f] for i in range(size)], axis=0)
            part = lax.dot_general(lhs, full[f], ROWS_LAST, preferred_element_type=jnp.float32)
            total = part if total is None else total + part
        found[pl.ds(base * count, size * count)] = total
        for tile in range(2 * base, 2 * (base + size)):

            @pl.when(place_ref[tile] >= 0)
            def _(tile=tile):
                out_copy(tile).start()

        base += size
    for tile in range(2 * pieces):

        @pl.when(place_ref[tile] >= 0)
        def _(tile=tile):
            out_copy(tile).wait()


def tiles(place, near, far, groups, shape, out=None):
    parts, wide, depth = near.shape
    sizes = tuple(len(group) for group in groups)
    pieces = [half for group in groups for piece in group for half in piece]
    number = len(pieces) // 2
    count = pieces[0].shape[1]
    anywhere = pl.BlockSpec(memory_space=pl.ANY)
    given = [place, near, far, *pieces] + ([] if out is None else [out])
    return pl.pallas_call(
        functools.partial(tiles_kernel, sizes, 0 if out is None else 1),
        in_specs=[pl.BlockSpec(memory_space=pltpu.SMEM)] + [anywhere] * (len(given) - 1),
        out_specs=anywhere,
        out_shape=jax.ShapeDtypeStruct(shape, jnp.float32),
        input_output_aliases={} if out is None else {len(given) - 1: 0},
        scratch_shapes=[
            pltpu.VMEM((2 * parts, wide, depth), near.dtype),
            pltpu.VMEM((number, 2 * parts, count, depth), near.dtype),
            pltpu.VMEM((number * count, wide), jnp.float32),
            pltpu.SemaphoreType.DMA((2 * parts,)),
            pltpu.SemaphoreType.DMA((2 * number,)),
            pltpu.SemaphoreType.DMA((2 * number,)),
        ],
        compiler_params=pltpu.CompilerParams(vmem_limit_bytes=52 * 1024 * 1024),
        cost_estimate=pl.CostEstimate(
            flops=4 * parts * wide * depth * number * count,
            bytes_accessed=4 * parts * depth * (wide + number * count) + 4 * number * count * wide,
            transcendentals=0,
        ),
    )(*given)


def half_kernel(final, *refs):
    place_ref, refs = (refs[0], refs[1:]) if final else (None, refs)
    full_ref, here_ref, there_ref = refs[:3]
    sums_ref = refs[3] if final else None
    out_ref = refs[5] if final else refs[3]
    full, held, found, sums, full_sem, held_sem, sums_sem, out_sem = refs[6 if final else 4 :]
    parts, count = full.shape[0], held.shape[1] // 2
    rows = count // 2

    full_copies = [pltpu.make_async_copy(full_ref.at[f], full.at[f], full_sem.at[f]) for f in range(parts)]
    held_copies = [
        pltpu.make_async_copy(ref.at[f], held.at[f, pl.ds(i * count, count)], held_sem.at[i * parts + f])
        for i, ref in enumerate((here_ref, there_ref))
        for f in range(parts)
    ]
    for f in range(parts):
        for copy in (full_copies[f], held_copies[f], held_copies[parts + f]):
            copy.start()
    if final:
        sums_copy = pltpu.make_async_copy(sums_ref, sums, sums_sem)
        sums_copy.start()
    total = None
    for f in range(parts):
        for copy in (full_copies[f], held_copies[f], held_copies[parts + f]):
            copy.wait()
        part = lax.dot_general(held[f], full[f], ROWS_LAST, preferred_element_type=jnp.float32)
        total = part if total is None else total + part
    if final:
        sums_copy.wait()
        found[...] = total + sums[...]
        for tile in range(4):
            copy = pltpu.make_async_copy(
                found.at[pl.ds(tile * rows, rows)], out_ref.at[place_ref[tile]], out_sem.at[tile]
            )
            copy.start()
        for tile in range(4):
            copy = pltpu.make_async_copy(
                found.at[pl.ds(tile * rows, rows)], out_ref.at[place_ref[tile]], out_sem.at[tile]
            )
            copy.wait()
    else:
        found[...] = total
        copy = pltpu.make_async_copy(found, out_ref, sums_sem)
        copy.start()
        copy.wait()


def half_tiles(full, pieces, place=None, sums=None, out=None):
    parts, wide, depth = full.shape
    count = 2 * pieces[0].shape[1]
    final = out is not None
    anywhere = pl.BlockSpec(memory_space=pl.ANY)
    given = [place, full, *pieces, sums, out] if final else [full, *pieces]
    specs = [anywhere] * len(given)
    if final:
        specs[0] = pl.BlockSpec(memory_space=pltpu.SMEM)
    shape = out.shape if final else (count, wide)
    return pl.pallas_call(
        functools.partial(half_kernel, final),
        in_specs=specs,
        out_specs=anywhere,
        out_shape=jax.ShapeDtypeStruct(shape, jnp.float32),
        input_output_aliases={5: 0} if final else {},
        scratch_shapes=[
            pltpu.VMEM((parts, wide, depth), full.dtype),
            pltpu.VMEM((parts, count, depth), full.dtype),
            pltpu.VMEM((count, wide), jnp.float32),
            pltpu.VMEM((count, wide), jnp.float32),
            pltpu.SemaphoreType.DMA((parts,)),
            pltpu.SemaphoreType.DMA((2 * parts,)),
            pltpu.SemaphoreType.DMA,
            pltpu.SemaphoreType.DMA((4,)),
        ],
        compiler_params=pltpu.CompilerParams(vmem_limit_bytes=52 * 1024 * 1024),
        cost_estimate=pl.CostEstimate(
            flops=2 * parts * wide * depth * count,
            bytes_accessed=2 * parts * depth * (wide + count) + 4 * count * wide,
            transcendentals=0,
        ),
    )(*given)


def per_device(examples):
    blocks = lax.axis_size("ex")
    feats = lax.axis_size("feat")
    half = blocks // 2
    steps = blocks // 8
    ex = lax.axis_index("ex")
    core = ex % 2
    rows, depth = examples.shape
    line = feats // 2
    lines = [[q * line + x for x in range(line)] for q in range(2)]

    swap_pairs = [(i, i ^ 1) for i in range(blocks)]
    first_pairs = [(i, i - 2) for i in range(blocks) if i % 2 == 0 and i % half != 0]
    first_pairs += [(i, (i + half) % blocks) for i in range(blocks) if i % 2 == 1]
    wrap_pairs = [(1, half - 2), (half + 1, blocks - 2)]
    later_pairs = [(i, (i - 2 if i % 2 == 0 else i + 2) % blocks) for i in range(blocks)]
    wraps = (core == 0) & (ex % half == half - 2)

    def swap(piece):
        return lax.ppermute(piece, "ex", swap_pairs)

    near = lax.all_gather(examples, "feat", axis=0, axis_index_groups=lines)
    facing = lax.ppermute(examples, "feat", [(f, (f + line) % feats) for f in range(feats)])
    own = lax.all_to_all(examples.reshape(feats, rows // feats, depth), "feat", 0, 0)
    first = lax.axis_index("feat") < line
    own = after(own, facing)
    own_halves = [jnp.where(first, own[:line], own[line:]), jnp.where(first, own[line:], own[:line])]
    start = [jnp.concatenate([piece, swap(piece)], axis=1) for piece in own_halves]

    spots = [jnp.where(core == 0, 0, 1), jnp.where(core == 0, 1, 0)]
    for step in range(1, steps + 1):
        low, high = 2 * step, half + 2 - 2 * step
        mine, theirs = jnp.where(core == 0, low, high), jnp.where(core == 0, high, low)
        spots += [mine + core, mine + 1 - core, theirs + 1 - core, theirs + core]
    place = jnp.stack([jnp.where(spot - core > half, -1, spot - core) for spot in spots]).astype(jnp.int32)
    shape = (half + 1, rows // feats, rows)
    split = 2 + 4 * (steps - 1)

    turn = rows // feats
    held = start
    groups = [[start]]
    for step in range(steps):
        if step == 2:
            held = [after(held[0], near), held[1]]
        if step == steps - 1:
            early = 2 + 4 * (steps - 2)
            out = tiles(place[:early], near, far, groups[:-1], shape)
            held = [held[0], after(held[1], out)]
        held = [lax.ppermute(piece, "ex", first_pairs if step == 0 else later_pairs) for piece in held]
        if step == 0:
            wrapped = [lax.ppermute(piece, "ex", wrap_pairs) for piece in held]
            held = [
                jnp.where(wraps, jnp.concatenate([new[:, turn:], new[:, :turn]], axis=1), piece)
                for new, piece in zip(wrapped, held)
            ]
            far = lax.all_gather(facing, "feat", axis=0, axis_index_groups=lines)
        if step == steps - 1:
            across = swap(held[1])
            out = tiles(place[early:split], near, far, groups[-1:], shape, out)
            sums = half_tiles(far, [held[1], across])
            last = after(held[0], out)
            return half_tiles(near, [last, swap(last)], place[split:], sums, out)
        groups.append([held, [swap(piece) for piece in held]])


def solution(mesh):
    placed = (P("ex", "feat"),)
    return jax.shard_map(
        per_device,
        mesh=mesh,
        in_specs=placed,
        out_specs=P(None, ("ex", "feat"), None),
        check_vma=False,
    )
```

```python
import functools

import jax
import jax.numpy as jnp
from jax import lax
from jax.experimental import pallas as pl
from jax.experimental.pallas import tpu as pltpu
from jax.sharding import PartitionSpec as P

ROWS_LAST = (((1,), (1,)), ((), ()))


def after(value, *others):
    return lax.optimization_barrier((value, *others))[0]


def tiles_kernel(sizes, aliased, place_ref, *refs):
    pieces = sum(sizes)
    full_refs, piece_refs = refs[:2], refs[2 : 2 + 2 * pieces]
    out_ref = refs[2 + 2 * pieces + aliased]
    full, held, found, full_sem, held_sem, out_sem = refs[3 + 2 * pieces + aliased :]
    parts = full_refs[0].shape[0]
    count = held.shape[2]
    rows = count // 2

    full_copies = [
        pltpu.make_async_copy(full_refs[h].at[f], full.at[h * parts + f], full_sem.at[h * parts + f])
        for h in range(2)
        for f in range(parts)
    ]
    held_copies = [
        pltpu.make_async_copy(piece_refs[2 * i + h], held.at[i, pl.ds(h * parts, parts)], held_sem.at[2 * i + h])
        for i in range(pieces)
        for h in range(2)
    ]
    first = 2 * sizes[0]
    full_copies[0].start()
    for copy in held_copies[:first:2]:
        copy.start()
    for copy in full_copies[1:parts]:
        copy.start()
    for copy in held_copies[1:first:2]:
        copy.start()
    for copy in full_copies[parts:] + held_copies[first:]:
        copy.start()

    def out_copy(tile):
        return pltpu.make_async_copy(found.at[pl.ds(tile * rows, rows)], out_ref.at[place_ref[tile]], out_sem.at[tile])

    base = 0
    for g, size in enumerate(sizes):
        total = None
        for f in range(2 * parts):
            if g == 0:
                full_copies[f].wait()
            if f % parts == 0:
                for copy in held_copies[2 * base + f // parts : 2 * (base + size) : 2]:
                    copy.wait()
            lhs = jnp.concatenate([held[base + i, f] for i in range(size)], axis=0)
            part = lax.dot_general(lhs, full[f], ROWS_LAST, preferred_element_type=jnp.float32)
            total = part if total is None else total + part
        found[pl.ds(base * count, size * count)] = total
        for tile in range(2 * base, 2 * (base + size)):

            @pl.when(place_ref[tile] >= 0)
            def _(tile=tile):
                out_copy(tile).start()

        base += size
    for tile in range(2 * pieces):

        @pl.when(place_ref[tile] >= 0)
        def _(tile=tile):
            out_copy(tile).wait()


def tiles(place, near, far, groups, shape, out=None):
    parts, wide, depth = near.shape
    sizes = tuple(len(group) for group in groups)
    pieces = [half for group in groups for piece in group for half in piece]
    number = len(pieces) // 2
    count = pieces[0].shape[1]
    anywhere = pl.BlockSpec(memory_space=pl.ANY)
    given = [place, near, far, *pieces] + ([] if out is None else [out])
    return pl.pallas_call(
        functools.partial(tiles_kernel, sizes, 0 if out is None else 1),
        in_specs=[pl.BlockSpec(memory_space=pltpu.SMEM)] + [anywhere] * (len(given) - 1),
        out_specs=anywhere,
        out_shape=jax.ShapeDtypeStruct(shape, jnp.float32),
        input_output_aliases={} if out is None else {len(given) - 1: 0},
        scratch_shapes=[
            pltpu.VMEM((2 * parts, wide, depth), near.dtype),
            pltpu.VMEM((number, 2 * parts, count, depth), near.dtype),
            pltpu.VMEM((number * count, wide), jnp.float32),
            pltpu.SemaphoreType.DMA((2 * parts,)),
            pltpu.SemaphoreType.DMA((2 * number,)),
            pltpu.SemaphoreType.DMA((2 * number,)),
        ],
        compiler_params=pltpu.CompilerParams(vmem_limit_bytes=52 * 1024 * 1024),
        cost_estimate=pl.CostEstimate(
            flops=4 * parts * wide * depth * number * count,
            bytes_accessed=4 * parts * depth * (wide + number * count) + 4 * number * count * wide,
            transcendentals=0,
        ),
    )(*given)


def half_kernel(final, *refs):
    place_ref, refs = (refs[0], refs[1:]) if final else (None, refs)
    full_ref, here_ref, there_ref = refs[:3]
    sums_ref = refs[3] if final else None
    out_ref = refs[5] if final else refs[3]
    full, held, found, sums, full_sem, held_sem, sums_sem, out_sem = refs[6 if final else 4 :]
    parts, count = full.shape[0], held.shape[1] // 2
    rows = count // 2

    full_copies = [pltpu.make_async_copy(full_ref.at[f], full.at[f], full_sem.at[f]) for f in range(parts)]
    held_copies = [
        pltpu.make_async_copy(ref.at[f], held.at[f, pl.ds(i * count, count)], held_sem.at[i * parts + f])
        for i, ref in enumerate((here_ref, there_ref))
        for f in range(parts)
    ]
    for f in range(parts):
        for copy in (full_copies[f], held_copies[f], held_copies[parts + f]):
            copy.start()
    if final:
        sums_copy = pltpu.make_async_copy(sums_ref, sums, sums_sem)
        sums_copy.start()
    total = None
    for f in range(parts):
        for copy in (full_copies[f], held_copies[f], held_copies[parts + f]):
            copy.wait()
        part = lax.dot_general(held[f], full[f], ROWS_LAST, preferred_element_type=jnp.float32)
        total = part if total is None else total + part
    if final:
        sums_copy.wait()
        found[...] = total + sums[...]
        for tile in range(4):
            copy = pltpu.make_async_copy(
                found.at[pl.ds(tile * rows, rows)], out_ref.at[place_ref[tile]], out_sem.at[tile]
            )
            copy.start()
        for tile in range(4):
            copy = pltpu.make_async_copy(
                found.at[pl.ds(tile * rows, rows)], out_ref.at[place_ref[tile]], out_sem.at[tile]
            )
            copy.wait()
    else:
        found[...] = total
        copy = pltpu.make_async_copy(found, out_ref, sums_sem)
        copy.start()
        copy.wait()


def half_tiles(full, pieces, place=None, sums=None, out=None):
    parts, wide, depth = full.shape
    count = 2 * pieces[0].shape[1]
    final = out is not None
    anywhere = pl.BlockSpec(memory_space=pl.ANY)
    given = [place, full, *pieces, sums, out] if final else [full, *pieces]
    specs = [anywhere] * len(given)
    if final:
        specs[0] = pl.BlockSpec(memory_space=pltpu.SMEM)
    shape = out.shape if final else (count, wide)
    return pl.pallas_call(
        functools.partial(half_kernel, final),
        in_specs=specs,
        out_specs=anywhere,
        out_shape=jax.ShapeDtypeStruct(shape, jnp.float32),
        input_output_aliases={5: 0} if final else {},
        scratch_shapes=[
            pltpu.VMEM((parts, wide, depth), full.dtype),
            pltpu.VMEM((parts, count, depth), full.dtype),
            pltpu.VMEM((count, wide), jnp.float32),
            pltpu.VMEM((count, wide), jnp.float32),
            pltpu.SemaphoreType.DMA((parts,)),
            pltpu.SemaphoreType.DMA((2 * parts,)),
            pltpu.SemaphoreType.DMA,
            pltpu.SemaphoreType.DMA((4,)),
        ],
        compiler_params=pltpu.CompilerParams(vmem_limit_bytes=52 * 1024 * 1024),
        cost_estimate=pl.CostEstimate(
            flops=2 * parts * wide * depth * count,
            bytes_accessed=2 * parts * depth * (wide + count) + 4 * count * wide,
            transcendentals=0,
        ),
    )(*given)


def per_device(examples):
    blocks = lax.axis_size("ex")
    feats = lax.axis_size("feat")
    half = blocks // 2
    steps = blocks // 8
    ex = lax.axis_index("ex")
    core = ex % 2
    rows, depth = examples.shape
    line = feats // 2
    lines = [[q * line + x for x in range(line)] for q in range(2)]

    swap_pairs = [(i, i ^ 1) for i in range(blocks)]
    first_pairs = [(i, i - 2) for i in range(blocks) if i % 2 == 0 and i % half != 0]
    first_pairs += [(i, (i + half) % blocks) for i in range(blocks) if i % 2 == 1]
    wrap_pairs = [(1, half - 2), (half + 1, blocks - 2)]
    later_pairs = [(i, (i - 2 if i % 2 == 0 else i + 2) % blocks) for i in range(blocks)]
    wraps = (core == 0) & (ex % half == half - 2)

    def swap(piece):
        return lax.ppermute(piece, "ex", swap_pairs)

    near = lax.all_gather(examples, "feat", axis=0, axis_index_groups=lines)
    facing = lax.ppermute(examples, "feat", [(f, (f + line) % feats) for f in range(feats)])
    own = lax.all_to_all(examples.reshape(feats, rows // feats, depth), "feat", 0, 0)
    first = lax.axis_index("feat") < line
    own = after(own, facing)
    own_halves = [jnp.where(first, own[:line], own[line:]), jnp.where(first, own[line:], own[:line])]
    start = [jnp.concatenate([piece, swap(piece)], axis=1) for piece in own_halves]

    spots = [jnp.where(core == 0, 0, 1), jnp.where(core == 0, 1, 0)]
    for step in range(1, steps + 1):
        low, high = 2 * step, half + 2 - 2 * step
        mine, theirs = jnp.where(core == 0, low, high), jnp.where(core == 0, high, low)
        spots += [mine + core, mine + 1 - core, theirs + 1 - core, theirs + core]
    place = jnp.stack([jnp.where(spot - core > half, -1, spot - core) for spot in spots]).astype(jnp.int32)
    shape = (half + 1, rows // feats, rows)
    split = 2 + 4 * (steps - 1)

    turn = rows // feats
    held = start
    groups = [[start]]
    for step in range(steps):
        if step == steps - 1:
            early = 2 + 4 * (steps - 2)
            out = tiles(place[:early], near, far, groups[:-1], shape)
            held = [held[0], after(held[1], out)]
        held = [lax.ppermute(piece, "ex", first_pairs if step == 0 else later_pairs) for piece in held]
        if step == 0:
            wrapped = [lax.ppermute(piece, "ex", wrap_pairs) for piece in held]
            held = [
                jnp.where(wraps, jnp.concatenate([new[:, turn:], new[:, :turn]], axis=1), piece)
                for new, piece in zip(wrapped, held)
            ]
            far = lax.all_gather(facing, "feat", axis=0, axis_index_groups=lines)
        if step == steps - 1:
            across = swap(held[1])
            out = tiles(place[early:split], near, far, groups[-1:], shape, out)
            sums = half_tiles(far, [held[1], across])
            last = after(held[0], out)
            return half_tiles(near, [last, swap(last)], place[split:], sums, out)
        groups.append([held, [swap(piece) for piece in held]])


def solution(mesh):
    placed = (P("ex", "feat"),)
    return jax.shard_map(
        per_device,
        mesh=mesh,
        in_specs=placed,
        out_specs=P(None, ("ex", "feat"), None),
        check_vma=False,
    )
```
